512 devices in a mesh: grp: 32 (over z, x_lo, core), rep: 16 (over y, x_hi).
Axes of the slice: x: 4 (x_hi: 2, x_lo: 2; x = x_hi * 2 + x_lo), y: 8, z: 8, core: 2. Of those that a mesh axis runs over, the one named last changes fastest.
Arguments:
- embeddings: bfloat16 [16, 8192, 512], P('rep', 'grp'), may hold values from -64 to 64
- cluster_of: int32 [16, 8192], P('rep', 'grp'), may hold values from 0 to 7, as said below
- cluster_rows: int32 [16, 2, 8], P('rep'), may hold values from 0 to 8192, as said below
Outputs:
- max_similarity: float32 [16, 8192], P('rep', 'grp')
The draws below stay inside these ranges and needn't reach their ends.
Inputs may be any that keep to these rules, and one draw needn't show every extreme that they name: Along a set's rows cluster_of never falls; cluster c occupies exactly the rows cluster_rows[s, 0, c] to cluster_rows[s, 1, c] - 1, and holds at least 2 rows. `cluster_rows`: the clusters of a set tile its rows in order: cluster 0 starts at row 0, each cluster starts where the previous one ends, the last ends at 8192.
All inputs are finite; a program needn't handle non-finite values.
Results may differ from the reference program's by a relative error of at most 0.00043.
Values may be sent and summed in bfloat16 or wider, within the bound.
No kernel may reach another device: no remote copies, remote signals or barrier semaphores. Data moves between devices by JAX's collectives and lax.ppermute only.
A program may use at most 64 MiB of HBM per device.

```python
import jax
import jax.numpy as jnp
from jax import lax

D = 512
ROWS = 256
CLUSTERS = 8
SETROWS = 8192
N_GRP = 32
N_REP = 16


def cluster_layout(key):
    ranks = jax.vmap(lambda one_key: jax.random.permutation(one_key, CLUSTERS))(jax.random.split(key, N_REP)).astype(jnp.int32) + 1
    factor = jax.random.randint(jax.random.fold_in(key, 1), (N_REP, CLUSTERS), 2, 5).astype(jnp.int32)
    biggest = SETROWS // 2 + SETROWS // 8
    weight = jnp.where(ranks == 1, 0, 16384 // ranks * factor)
    spare = SETROWS - biggest - 2 * (CLUSTERS - 1)
    share = weight * spare // jnp.sum(weight, axis=1, keepdims=True)
    sizes = jnp.where(ranks == 1, biggest, 2 + share)
    leftover = SETROWS - jnp.sum(sizes, axis=1, keepdims=True)
    sizes = sizes + jnp.where(ranks == 1, leftover, 0)
    ends = jnp.cumsum(sizes, axis=1).astype(jnp.int32)
    starts = ends - sizes
    row_index = jnp.arange(SETROWS, dtype=jnp.int32)
    member_of = jnp.sum((ends[:, None, :] <= row_index[None, :, None]).astype(jnp.int32), axis=2).astype(jnp.int32)
    return (member_of, starts, ends)


def draw_cluster_of(key, part):
    member_of, starts, ends = cluster_layout(key)
    return member_of


def draw_cluster_rows(key, part):
    member_of, starts, ends = cluster_layout(key)
    return jnp.stack([starts, ends], axis=1).astype(jnp.int32)


def draw_embeddings(key, part):
    member_of, starts, ends = cluster_layout(key)
    key = jax.random.fold_in(key, 11)
    keys = jax.random.split(key, 5)
    common = jax.random.normal(keys[0], (D,), jnp.float32)
    centers = jax.random.normal(keys[1], (N_REP, CLUSTERS, D), jnp.float32)
    member_centers = jax.vmap(lambda table, index: table[index])(centers, member_of)
    place = (jnp.arange(N_REP * SETROWS, dtype=jnp.float32) / (N_REP * SETROWS - 1)).reshape(N_REP, SETROWS, 1)
    column = jnp.exp(jax.random.uniform(keys[4], (D,), jnp.float32, 0.0, 2.302585)) / 3.0
    noise = jax.random.normal(keys[2], (N_REP, SETROWS, D), jnp.float32)
    rise = 1.0 + 2.0 * place
    scale = jnp.exp(jax.random.uniform(keys[3], (N_REP, SETROWS, 1), jnp.float32, 0.0, 2.302585))
    strength = 1.2
    values = scale * (rise * common + strength * member_centers + noise) * column
    return (64.0 * jnp.tanh(values / 64.0)).astype(jnp.bfloat16)


def setup_inputs(seed: int = 0) -> dict:
    arg_keys = jax.random.split(jax.random.key(seed), 4)
    return {
        "embeddings": draw_embeddings(jax.random.fold_in(arg_keys[3], 71), 0),
        "cluster_of": draw_cluster_of(jax.random.fold_in(arg_keys[3], 71), 0),
        "cluster_rows": draw_cluster_rows(jax.random.fold_in(arg_keys[3], 71), 0),
    }


def reference(embeddings, cluster_of, cluster_rows):
    values = embeddings.astype(jnp.float32)
    set_rows = values.shape[1]
    centroid = lax.optimization_barrier(jnp.sum(values, axis=(0, 1))) / (values.shape[0] * set_rows)
    centered = values - centroid
    unit_rows = (centered * lax.rsqrt(lax.optimization_barrier(jnp.sum(centered * centered, axis=2, keepdims=True)) + 1e-06)).astype(jnp.bfloat16)
    first_row = jnp.take_along_axis(cluster_rows[:, 0, :], cluster_of, axis=1)
    end_row = jnp.take_along_axis(cluster_rows[:, 1, :], cluster_of, axis=1)

    def one_set(operands):
        unit_set, first_set, end_set = operands
        columns = jnp.arange(set_rows, dtype=jnp.int32)

        def one_block(index):
            start = (index * ROWS).astype(jnp.int32)
            block = lax.dynamic_slice_in_dim(unit_set, start, ROWS, 0)
            first_block = lax.dynamic_slice_in_dim(first_set, start, ROWS, 0)
            end_block = lax.dynamic_slice_in_dim(end_set, start, ROWS, 0)
            position = start + jnp.arange(ROWS, dtype=jnp.int32)
            scores = jnp.dot(block, unit_set.T, preferred_element_type=jnp.float32)
            inside = (columns[None, :] >= first_block[:, None]) & (columns[None, :] < end_block[:, None]) & (columns[None, :] != position[:, None])
            return lax.optimization_barrier(jnp.max(jnp.where(inside, scores, jnp.float32(-2.0)), axis=1))
        return lax.map(one_block, jnp.arange(N_GRP, dtype=jnp.int32)).reshape(set_rows)
    return lax.map(one_set, (unit_rows, first_row, end_row))
```

```python
import functools

import jax
import jax.numpy as jnp
from jax import lax
from jax.experimental import pallas as pl
from jax.experimental.pallas import tpu as pltpu
from jax.sharding import Mesh, PartitionSpec as P

Z, XL, C, Y, XH = 8, 2, 2, 8, 2
GRP = ("z", "xl", "c")
REP = ("y", "xh")
ROWS = 256
CHIP = C * ROWS
PLANE = XL * CHIP
D = 512
TOTAL = Z * PLANE * Y * XH
NONE = -2.0
STEP = 256


def shift(hops):
    return [(z * C + c, (z + hops[c]) % Z * C + c) for z in range(Z) for c in range(C)]


def spread_sum(partial, axes, count):
    return lax.all_to_all(jnp.broadcast_to(partial[None], (count, 4, 128)), axes, 0, 0)


def score_kernel(
    bounds, partials, own, chip, side, two, odd, four, out, rows, cols, unit, sems
):
    z, xl, core = lax.axis_index("z"), lax.axis_index("xl"), lax.axis_index("c")
    sign = 2 * core - 1
    here = pl.multiple_of(xl * CHIP, CHIP)
    there = pl.multiple_of((1 - xl) * CHIP, CHIP)
    copies = [
        pltpu.make_async_copy(chip, rows.at[pl.ds(here, CHIP)], sems.at[0]),
        pltpu.make_async_copy(side, rows.at[pl.ds(there, CHIP)], sems.at[1]),
        pltpu.make_async_copy(own, cols.at[pl.ds(0, ROWS)], sems.at[2]),
        pltpu.make_async_copy(two, cols.at[pl.ds(ROWS, CHIP)], sems.at[3]),
        pltpu.make_async_copy(odd, cols.at[pl.ds(ROWS + CHIP, 2 * CHIP)], sems.at[4]),
        pltpu.make_async_copy(four, cols.at[pl.ds(ROWS + 3 * CHIP, ROWS)], sems.at[5]),
    ]
    for copy in copies:
        copy.start()
    total = jnp.sum(partials[...], axis=0)
    centroid = jnp.concatenate([total[k : k + 1] for k in range(4)], axis=1) / TOTAL

    def normalized(block):
        centered = block.astype(jnp.float32) - centroid
        norm = jnp.sum(centered * centered, axis=1, keepdims=True)
        return (centered * lax.rsqrt(norm + 1e-06)).astype(jnp.bfloat16)

    def cluster(position):
        member = jnp.zeros(position.shape, jnp.int32)
        for k in range(7):
            member += (position >= bounds[0, 1, k]).astype(jnp.int32)
        return member

    copies[0].wait()
    copies[1].wait()
    for k in range(PLANE // STEP):
        unit[pl.ds(k * STEP, STEP)] = normalized(rows[pl.ds(k * STEP, STEP)])
    row_position = z * PLANE + lax.broadcasted_iota(jnp.int32, (1, PLANE), 1)
    row_cluster = cluster(row_position)

    def plane_start(offset):
        return lax.rem(z + offset + Z, Z) * PLANE + xl * CHIP

    starts = [plane_start(0) + core * ROWS]
    for offset in (2 * sign, sign, 3 * sign):
        starts += [plane_start(offset), plane_start(offset) + ROWS]
    starts += [plane_start(4) + core * ROWS]
    waits = {0: 2, 1: 3, 3: 4, 7: 5}
    best = jnp.full((8, PLANE), NONE, jnp.float32)
    for k, start in enumerate(starts):
        if k in waits:
            copies[waits[k]].wait()
        piece = normalized(cols[pl.ds(k * STEP, STEP)])
        scores = lax.dot_general(
            piece, unit[...], (((1,), (1,)), ((), ())), preferred_element_type=jnp.float32
        )
        position = start + lax.broadcasted_iota(jnp.int32, (STEP, 1), 0)
        inside = cluster(position) == row_cluster
        if k == 0:
            inside &= position != row_position
        scores = jnp.where(inside, scores, NONE)
        best = jnp.maximum(best, jnp.max(scores.reshape(STEP // 8, 8, PLANE), axis=0))
    best = jnp.max(best, axis=0, keepdims=True)
    for k in range(PLANE // 128):
        out[k // 2, pl.ds(k % 2, 1)] = best[:, k * 128 : (k + 1) * 128]


def score(bounds, partials, *blocks):
    return pl.pallas_call(
        score_kernel,
        out_shape=jax.ShapeDtypeStruct((XL * C, ROWS // 128, 128), jnp.float32),
        in_specs=[
            pl.BlockSpec(memory_space=pltpu.SMEM),
            pl.BlockSpec(memory_space=pltpu.VMEM),
        ]
        + [pl.BlockSpec(memory_space=pl.ANY)] * len(blocks),
        out_specs=pl.BlockSpec(memory_space=pltpu.VMEM),
        scratch_shapes=[
            pltpu.VMEM((PLANE, D), jnp.bfloat16),
            pltpu.VMEM((2 * PLANE, D), jnp.bfloat16),
            pltpu.VMEM((PLANE, D), jnp.bfloat16),
            pltpu.SemaphoreType.DMA((6,)),
        ],
        compiler_params=pltpu.CompilerParams(vmem_limit_bytes=32 * 1024 * 1024),
        cost_estimate=pl.CostEstimate(
            flops=2 * PLANE * 2 * PLANE * D, bytes_accessed=3 * PLANE * D * 2, transcendentals=0
        ),
        name="score",
    )(bounds, partials, *blocks)


def on_device(embeddings, cluster_rows):
    own = embeddings[0]
    chip = lax.all_gather(own, "c", axis=0, tiled=True)
    two = lax.ppermute(chip, ("z", "c"), shift((2, -2)))
    side = lax.ppermute(chip, "xl", [(0, 1), (1, 0)])
    column_sums = jnp.sum(chip, axis=0, dtype=jnp.float32).reshape(4, 128)
    set_sums = jnp.sum(spread_sum(column_sums, ("z", "xl"), Z * XL), axis=0)
    two, set_sums = lax.optimization_barrier((two, set_sums))
    odd = lax.ppermute(jnp.concatenate([chip, two], axis=0), ("z", "c"), shift((1, -1)))
    half = lax.dynamic_slice_in_dim(two, lax.axis_index("c") * ROWS, ROWS, 0)
    four = lax.ppermute(half, ("z", "c"), shift((2, -2)))
    partials = spread_sum(set_sums, REP, Y * XH)
    best = score(cluster_rows, partials, own, chip, side, two, odd, four)
    best = lax.all_to_all(best, ("xl", "c"), 0, 0)
    return jnp.max(best, axis=0).reshape(1, ROWS)


def solution(mesh):
    fine = Mesh(mesh.devices.reshape(Z, XL, C, Y, XH), (*GRP, *REP))
    inner = jax.shard_map(
        on_device,
        mesh=fine,
        in_specs=(P(REP, GRP, None), P(REP, None, None)),
        out_specs=P(REP, GRP),
        check_vma=False,
    )

    def run(embeddings, cluster_of, cluster_rows):
        del cluster_of
        return inner(embeddings, cluster_rows)

    return run
```

```python
import jax
import jax.numpy as jnp
from jax import lax
from jax.experimental import pallas as pl
from jax.experimental.pallas import tpu as pltpu
from jax.sharding import Mesh, PartitionSpec as P

Z, XL, C, Y, XH = 8, 2, 2, 8, 2
GRP = ("z", "xl", "c")
REP = ("y", "xh")
ROWS = 256
CHIP = C * ROWS
PLANE = XL * CHIP
D = 512
TOTAL = Z * PLANE * Y * XH
NONE = -2.0
STEP = 256


def shift(hops):
    return [(z * C + c, (z + hops[c]) % Z * C + c) for z in range(Z) for c in range(C)]


def spread_sum(partial, axes, count):
    return lax.all_to_all(jnp.broadcast_to(partial[None], (count, 4, 128)), axes, 0, 0)


def plane_start(z, xl, offset):
    return lax.rem(z + offset + Z, Z) * PLANE + xl * CHIP


def normalizer(partials):
    total = jnp.sum(partials[...], axis=0)
    centroid = jnp.concatenate([total[k : k + 1] for k in range(4)], axis=1) / TOTAL

    def normalized(block):
        centered = block.astype(jnp.float32) - centroid
        norm = jnp.sum(centered * centered, axis=1, keepdims=True)
        return (centered * lax.rsqrt(norm + 1e-06)).astype(jnp.bfloat16)

    return normalized


def cluster_by(bounds, position):
    member = jnp.zeros(position.shape, jnp.int32)
    for k in range(7):
        member += (position >= bounds[0, 1, k]).astype(jnp.int32)
    return member


def raise_best(best, bounds, unit, piece, start, z, diagonal=False):
    row_position = z * PLANE + lax.broadcasted_iota(jnp.int32, (1, PLANE), 1)
    scores = lax.dot_general(
        piece, unit[...], (((1,), (1,)), ((), ())), preferred_element_type=jnp.float32
    )
    position = start + lax.broadcasted_iota(jnp.int32, (STEP, 1), 0)
    inside = cluster_by(bounds, position) == cluster_by(bounds, row_position)
    if diagonal:
        inside &= position != row_position
    scores = jnp.where(inside, scores, NONE)
    return jnp.maximum(best, jnp.max(scores.reshape(STEP // 8, 8, PLANE), axis=0))


def near_kernel(
    bounds, partials, own, chip, side, two, one, unit, best, rows, cols, sems
):
    z, xl, core = lax.axis_index("z"), lax.axis_index("xl"), lax.axis_index("c")
    sign = 2 * core - 1
    here = pl.multiple_of(xl * CHIP, CHIP)
    there = pl.multiple_of((1 - xl) * CHIP, CHIP)
    copies = [
        pltpu.make_async_copy(chip, rows.at[pl.ds(here, CHIP)], sems.at[0]),
        pltpu.make_async_copy(side, rows.at[pl.ds(there, CHIP)], sems.at[1]),
        pltpu.make_async_copy(own, cols.at[pl.ds(0, ROWS)], sems.at[2]),
        pltpu.make_async_copy(two, cols.at[pl.ds(ROWS, CHIP)], sems.at[3]),
        pltpu.make_async_copy(one, cols.at[pl.ds(ROWS + CHIP, CHIP)], sems.at[4]),
    ]
    for copy in copies:
        copy.start()
    normalized = normalizer(partials)
    copies[0].wait()
    copies[1].wait()
    for k in range(PLANE // STEP):
        unit[pl.ds(k * STEP, STEP)] = normalized(rows[pl.ds(k * STEP, STEP)])
    starts = [plane_start(z, xl, 0) + core * ROWS]
    for offset in (2 * sign, sign):
        starts += [plane_start(z, xl, offset), plane_start(z, xl, offset) + ROWS]
    waits = {0: 2, 1: 3, 3: 4}
    found = jnp.full((8, PLANE), NONE, jnp.float32)
    for k, start in enumerate(starts):
        if k in waits:
            copies[waits[k]].wait()
        piece = normalized(cols[pl.ds(k * STEP, STEP)])
        found = raise_best(found, bounds, unit, piece, start, z, k == 0)
    best[...] = found


def far_kernel(bounds, partials, unit, best, three, four, out, cols, sems):
    z, xl, core = lax.axis_index("z"), lax.axis_index("xl"), lax.axis_index("c")
    sign = 2 * core - 1
    copies = [
        pltpu.make_async_copy(three, cols.at[pl.ds(0, CHIP)], sems.at[0]),
        pltpu.make_async_copy(four, cols.at[pl.ds(CHIP, ROWS)], sems.at[1]),
    ]
    for copy in copies:
        copy.start()
    normalized = normalizer(partials)
    starts = [plane_start(z, xl, 3 * sign), plane_start(z, xl, 3 * sign) + ROWS]
    starts += [plane_start(z, xl, 4) + core * ROWS]
    found = best[...]
    for k, start in enumerate(starts):
        if k == 0:
            copies[0].wait()
        if k == 2:
            copies[1].wait()
        piece = normalized(cols[pl.ds(k * STEP, STEP)])
        found = raise_best(found, bounds, unit, piece, start, z)
    found = jnp.max(found, axis=0, keepdims=True)
    for k in range(PLANE // 128):
        out[k // 2, pl.ds(k % 2, 1)] = found[:, k * 128 : (k + 1) * 128]


IN_VMEM = pl.BlockSpec(memory_space=pltpu.VMEM)
ANYWHERE = pl.BlockSpec(memory_space=pl.ANY)
PARAMS = pltpu.CompilerParams(vmem_limit_bytes=32 * 1024 * 1024)


def cost(flops):
    return pl.CostEstimate(flops=int(flops), bytes_accessed=4 * 2**20, transcendentals=0)


def near(bounds, partials, *blocks):
    return pl.pallas_call(
        near_kernel,
        out_shape=(
            jax.ShapeDtypeStruct((PLANE, D), jnp.bfloat16),
            jax.ShapeDtypeStruct((8, PLANE), jnp.float32),
        ),
        in_specs=[pl.BlockSpec(memory_space=pltpu.SMEM), IN_VMEM] + [ANYWHERE] * 5,
        out_specs=(IN_VMEM, IN_VMEM),
        scratch_shapes=[
            pltpu.VMEM((PLANE, D), jnp.bfloat16),
            pltpu.VMEM((ROWS + 2 * CHIP, D), jnp.bfloat16),
            pltpu.SemaphoreType.DMA((5,)),
        ],
        compiler_params=PARAMS,
        cost_estimate=cost(5e9),
        name="near",
    )(bounds, partials, *blocks)


def far(bounds, partials, unit, best, three, four):
    return pl.pallas_call(
        far_kernel,
        out_shape=jax.ShapeDtypeStruct((XL * C, ROWS // 128, 128), jnp.float32),
        in_specs=[pl.BlockSpec(memory_space=pltpu.SMEM)] + [IN_VMEM] * 3 + [ANYWHERE] * 2,
        out_specs=IN_VMEM,
        scratch_shapes=[
            pltpu.VMEM((CHIP + ROWS, D), jnp.bfloat16),
            pltpu.SemaphoreType.DMA((2,)),
        ],
        compiler_params=PARAMS,
        cost_estimate=cost(1e9),
        name="far",
    )(bounds, partials, unit, best, three, four)


def resend(received, count, flops):
    def kernel(received, out):
        total = jnp.sum(received[...], axis=0, keepdims=True)
        out[...] = jnp.broadcast_to(total, out.shape)

    return pl.pallas_call(
        kernel,
        out_shape=jax.ShapeDtypeStruct((count, 4, 128), jnp.float32),
        in_specs=[IN_VMEM],
        out_specs=IN_VMEM,
        cost_estimate=cost(flops),
        name="resend",
    )(received)


def on_device(embeddings, cluster_rows):
    own = embeddings[0]
    chip = lax.all_gather(own, "c", axis=0, tiled=True)
    two = lax.ppermute(chip, ("z", "c"), shift((2, -2)))
    one = lax.ppermute(chip, ("z", "c"), shift((1, -1)))
    side = lax.ppermute(chip, "xl", [(0, 1), (1, 0)])
    column_sums = jnp.sum(chip, axis=0, dtype=jnp.float32).reshape(4, 128)
    sums = spread_sum(column_sums, ("z", "xl", "xh"), Z * XL * XH)
    three = lax.ppermute(two, ("z", "c"), shift((1, -1)))
    sums = resend(sums, Y, 8000000000)
    half = lax.dynamic_slice_in_dim(three, lax.axis_index("c") * ROWS, ROWS, 0)
    four = lax.ppermute(half, ("z", "c"), shift((1, -1)))
    partials = lax.all_to_all(sums, "y", 0, 0)
    unit, best = near(cluster_rows, partials, own, chip, side, two, one)
    best = far(cluster_rows, partials, unit, best, three, four)
    best = lax.all_to_all(best, ("xl", "c"), 0, 0)
    return jnp.max(best, axis=0).reshape(1, ROWS)


def solution(mesh):
    fine = Mesh(mesh.devices.reshape(Z, XL, C, Y, XH), (*GRP, *REP))
    inner = jax.shard_map(
        on_device,
        mesh=fine,
        in_specs=(P(REP, GRP, None), P(REP, None, None)),
        out_specs=P(REP, GRP),
        check_vma=False,
    )

    def run(embeddings, cluster_of, cluster_rows):
        del cluster_of
        return inner(embeddings, cluster_rows)

    return run
```

```python
import jax
import jax.numpy as jnp
from jax import lax
from jax.experimental import pallas as pl
from jax.experimental.pallas import tpu as pltpu
from jax.sharding import Mesh, PartitionSpec as P

Z, XL, C, Y, XH = 8, 2, 2, 8, 2
GRP = ("z", "xl", "c")
REP = ("y", "xh")
ROWS = 256
CHIP = C * ROWS
PLANE = XL * CHIP
D = 512
TOTAL = Z * PLANE * Y * XH
NONE = -2.0
STEP = 256


def shift(hops):
    return [(z * C + c, (z + hops[c]) % Z * C + c) for z in range(Z) for c in range(C)]


def spread_sum(partial, axes, count):
    return lax.all_to_all(jnp.broadcast_to(partial[None], (count, 4, 128)), axes, 0, 0)


def plane_start(z, xl, offset):
    return lax.rem(z + offset + Z, Z) * PLANE + xl * CHIP


def normalizer(partials):
    total = jnp.sum(partials[...], axis=0)
    centroid = jnp.concatenate([total[k : k + 1] for k in range(4)], axis=1) / TOTAL

    def normalized(block):
        centered = block.astype(jnp.float32) - centroid
        norm = jnp.sum(centered * centered, axis=1, keepdims=True)
        return (centered * lax.rsqrt(norm + 1e-06)).astype(jnp.bfloat16)

    return normalized


def cluster_by(bounds, position):
    member = jnp.zeros(position.shape, jnp.int32)
    for k in range(7):
        member += (position >= bounds[0, 1, k]).astype(jnp.int32)
    return member


def raise_best(best, bounds, unit, piece, start, z, diagonal=False):
    row_position = z * PLANE + lax.broadcasted_iota(jnp.int32, (1, PLANE), 1)
    scores = lax.dot_general(
        piece, unit[...], (((1,), (1,)), ((), ())), preferred_element_type=jnp.float32
    )
    position = start + lax.broadcasted_iota(jnp.int32, (STEP, 1), 0)
    inside = cluster_by(bounds, position) == cluster_by(bounds, row_position)
    if diagonal:
        inside &= position != row_position
    scores = jnp.where(inside, scores, NONE)
    return jnp.maximum(best, jnp.max(scores.reshape(STEP // 8, 8, PLANE), axis=0))


def near_kernel(
    bounds, partials, own, chip, side, two, one, three, unit, best, rows, cols, sems
):
    z, xl, core = lax.axis_index("z"), lax.axis_index("xl"), lax.axis_index("c")
    sign = 2 * core - 1
    here = pl.multiple_of(xl * CHIP, CHIP)
    there = pl.multiple_of((1 - xl) * CHIP, CHIP)
    copies = [
        pltpu.make_async_copy(chip, rows.at[pl.ds(here, CHIP)], sems.at[0]),
        pltpu.make_async_copy(side, rows.at[pl.ds(there, CHIP)], sems.at[1]),
        pltpu.make_async_copy(own, cols.at[pl.ds(0, ROWS)], sems.at[2]),
        pltpu.make_async_copy(two, cols.at[pl.ds(ROWS, CHIP)], sems.at[3]),
        pltpu.make_async_copy(one, cols.at[pl.ds(ROWS + CHIP, CHIP)], sems.at[4]),
        pltpu.make_async_copy(three, cols.at[pl.ds(ROWS + 2 * CHIP, CHIP)], sems.at[5]),
    ]
    for copy in copies:
        copy.start()
    normalized = normalizer(partials)
    copies[0].wait()
    copies[1].wait()
    for k in range(PLANE // STEP):
        unit[pl.ds(k * STEP, STEP)] = normalized(rows[pl.ds(k * STEP, STEP)])
    starts = [plane_start(z, xl, 0) + core * ROWS]
    for offset in (2 * sign, sign, 3 * sign):
        starts += [plane_start(z, xl, offset), plane_start(z, xl, offset) + ROWS]
    waits = {0: 2, 1: 3, 3: 4, 5: 5}
    found = jnp.full((8, PLANE), NONE, jnp.float32)
    for k, start in enumerate(starts):
        if k in waits:
            copies[waits[k]].wait()
        piece = normalized(cols[pl.ds(k * STEP, STEP)])
        found = raise_best(found, bounds, unit, piece, start, z, k == 0)
    best[...] = found


def far_kernel(bounds, partials, unit, best, four, out):
    z, xl, core = lax.axis_index("z"), lax.axis_index("xl"), lax.axis_index("c")
    piece = normalizer(partials)(four[...])
    start = plane_start(z, xl, 4) + core * ROWS
    found = raise_best(best[...], bounds, unit, piece, start, z)
    found = jnp.max(found, axis=0, keepdims=True)
    for k in range(PLANE // 128):
        out[k // 2, pl.ds(k % 2, 1)] = found[:, k * 128 : (k + 1) * 128]


IN_VMEM = pl.BlockSpec(memory_space=pltpu.VMEM)
ANYWHERE = pl.BlockSpec(memory_space=pl.ANY)
PARAMS = pltpu.CompilerParams(vmem_limit_bytes=32 * 1024 * 1024)


def cost(flops):
    return pl.CostEstimate(flops=int(flops), bytes_accessed=4 * 2**20, transcendentals=0)


def near(bounds, partials, *blocks):
    return pl.pallas_call(
        near_kernel,
        out_shape=(
            jax.ShapeDtypeStruct((PLANE, D), jnp.bfloat16),
            jax.ShapeDtypeStruct((8, PLANE), jnp.float32),
        ),
        in_specs=[pl.BlockSpec(memory_space=pltpu.SMEM), IN_VMEM] + [ANYWHERE] * 6,
        out_specs=(IN_VMEM, IN_VMEM),
        scratch_shapes=[
            pltpu.VMEM((PLANE, D), jnp.bfloat16),
            pltpu.VMEM((ROWS + 3 * CHIP, D), jnp.bfloat16),
            pltpu.SemaphoreType.DMA((6,)),
        ],
        compiler_params=PARAMS,
        cost_estimate=cost(5e9),
        name="near",
    )(bounds, partials, *blocks)


def far(bounds, partials, unit, best, four):
    return pl.pallas_call(
        far_kernel,
        out_shape=jax.ShapeDtypeStruct((XL * C, ROWS // 128, 128), jnp.float32),
        in_specs=[pl.BlockSpec(memory_space=pltpu.SMEM)] + [IN_VMEM] * 4,
        out_specs=IN_VMEM,
        compiler_params=PARAMS,
        cost_estimate=cost(1e9),
        name="far",
    )(bounds, partials, unit, best, four)


def resend(received, count, flops):
    def kernel(received, out):
        total = jnp.sum(received[...], axis=0, keepdims=True)
        out[...] = jnp.broadcast_to(total, out.shape)

    return pl.pallas_call(
        kernel,
        out_shape=jax.ShapeDtypeStruct((count, 4, 128), jnp.float32),
        in_specs=[IN_VMEM],
        out_specs=IN_VMEM,
        compiler_params=pltpu.CompilerParams(vmem_limit_bytes=2 * 1024 * 1024),
        cost_estimate=cost(flops),
        name="resend",
    )(received)


def on_device(embeddings, cluster_rows):
    own = embeddings[0]
    chip = lax.all_gather(own, "c", axis=0, tiled=True)
    two = lax.ppermute(chip, ("z", "c"), shift((2, -2)))
    one = lax.ppermute(chip, ("z", "c"), shift((1, -1)))
    side = lax.ppermute(chip, "xl", [(0, 1), (1, 0)])
    column_sums = jnp.sum(chip, axis=0, dtype=jnp.float32).reshape(4, 128)
    sums = spread_sum(column_sums, ("z", "xl", "xh"), Z * XL * XH)
    three = lax.ppermute(two, ("z", "c"), shift((1, -1)))
    sums = resend(sums, Y, 8000000000)
    half = lax.dynamic_slice_in_dim(two, lax.axis_index("c") * ROWS, ROWS, 0)
    four = lax.ppermute(half, ("z", "c"), shift((2, -2)))
    partials = lax.all_to_all(sums, "y", 0, 0)
    unit, best = near(cluster_rows, partials, own, chip, side, two, one, three)
    best = far(cluster_rows, partials, unit, best, four)
    best = lax.all_to_all(best, ("xl", "c"), 0, 0)
    return jnp.max(best, axis=0).reshape(1, ROWS)


def solution(mesh):
    fine = Mesh(mesh.devices.reshape(Z, XL, C, Y, XH), (*GRP, *REP))
    inner = jax.shard_map(
        on_device,
        mesh=fine,
        in_specs=(P(REP, GRP, None), P(REP, None, None)),
        out_specs=P(REP, GRP),
        check_vma=False,
    )

    def run(embeddings, cluster_of, cluster_rows):
        del cluster_of
        return inner(embeddings, cluster_rows)

    return run
```

```python
import jax
import jax.numpy as jnp
from jax import lax
from jax.experimental import pallas as pl
from jax.experimental.pallas import tpu as pltpu
from jax.sharding import Mesh, PartitionSpec as P

Z, XL, C, Y, XH = 8, 2, 2, 8, 2
GRP = ("z", "xl", "c")
REP = ("y", "xh")
ROWS = 256
CHIP = C * ROWS
PLANE = XL * CHIP
D = 512
TOTAL = Z * PLANE * Y * XH
NONE = -2.0
STEP = 256


def shift(hops):
    return [(z * C + c, (z + hops[c]) % Z * C + c) for z in range(Z) for c in range(C)]


def spread_sum(partial, axes, count):
    return lax.all_to_all(jnp.broadcast_to(partial[None], (count, 4, 128)), axes, 0, 0)


def plane_start(z, xl, offset):
    return lax.rem(z + offset + Z, Z) * PLANE + xl * CHIP


def normalizer(partials):
    total = jnp.sum(partials[...], axis=0)
    centroid = jnp.concatenate([total[k : k + 1] for k in range(4)], axis=1) / TOTAL

    def normalized(block):
        centered = block.astype(jnp.float32) - centroid
        norm = jnp.sum(centered * centered, axis=1, keepdims=True)
        return (centered * lax.rsqrt(norm + 1e-06)).astype(jnp.bfloat16)

    return normalized


def cluster_by(bounds, position):
    member = jnp.zeros(position.shape, jnp.int32)
    for k in range(7):
        member += (position >= bounds[0, 1, k]).astype(jnp.int32)
    return member


def raise_best(best, bounds, unit, piece, start, z, diagonal=False):
    row_position = z * PLANE + lax.broadcasted_iota(jnp.int32, (1, PLANE), 1)
    scores = lax.dot_general(
        piece, unit[...], (((1,), (1,)), ((), ())), preferred_element_type=jnp.float32
    )
    position = start + lax.broadcasted_iota(jnp.int32, (STEP, 1), 0)
    inside = cluster_by(bounds, position) == cluster_by(bounds, row_position)
    if diagonal:
        inside &= position != row_position
    scores = jnp.where(inside, scores, NONE)
    return jnp.maximum(best, jnp.max(scores.reshape(STEP // 8, 8, PLANE), axis=0))


def near_kernel(
    bounds, partials, own, chip, side, two, one, three, unit, best, rows, cols, sems
):
    z, xl, core = lax.axis_index("z"), lax.axis_index("xl"), lax.axis_index("c")
    sign = 2 * core - 1
    here = pl.multiple_of(xl * CHIP, CHIP)
    there = pl.multiple_of((1 - xl) * CHIP, CHIP)
    copies = [
        pltpu.make_async_copy(chip, rows.at[pl.ds(here, CHIP)], sems.at[0]),
        pltpu.make_async_copy(side, rows.at[pl.ds(there, CHIP)], sems.at[1]),
        pltpu.make_async_copy(own, cols.at[pl.ds(0, ROWS)], sems.at[2]),
        pltpu.make_async_copy(two, cols.at[pl.ds(ROWS, CHIP)], sems.at[3]),
        pltpu.make_async_copy(one, cols.at[pl.ds(ROWS + CHIP, CHIP)], sems.at[4]),
        pltpu.make_async_copy(three, cols.at[pl.ds(ROWS + 2 * CHIP, CHIP)], sems.at[5]),
    ]
    for copy in copies:
        copy.start()
    normalized = normalizer(partials)
    starts = [plane_start(z, xl, 0) + core * ROWS]
    for offset in (2 * sign, sign, 3 * sign):
        starts += [plane_start(z, xl, offset), plane_start(z, xl, offset) + ROWS]
    waits = {0: 2, 1: 3, 3: 4, 5: 5}
    for k in range(len(starts)):
        if k in waits:
            copies[waits[k]].wait()
        block = pl.ds(k * STEP, STEP)
        cols[block] = normalized(cols[block])
    copies[0].wait()
    copies[1].wait()
    offset = lax.broadcasted_iota(jnp.int32, (STEP, 1), 0)
    col_cluster = [cluster_by(bounds, start + offset) for start in starts]
    for k in range(PLANE // STEP):
        block = pl.ds(k * STEP, STEP)
        slab = normalized(rows[block])
        unit[block] = slab
        position = z * PLANE + k * STEP + lax.broadcasted_iota(jnp.int32, (1, STEP), 1)
        row_cluster = cluster_by(bounds, position)
        scores = lax.dot_general(
            cols[...], slab, (((1,), (1,)), ((), ())), preferred_element_type=jnp.float32
        )
        found = jnp.full((8, STEP), NONE, jnp.float32)
        for j, start in enumerate(starts):
            inside = col_cluster[j] == row_cluster
            if j == 0:
                inside &= start + offset != position
            part = jnp.where(inside, scores[j * STEP : (j + 1) * STEP], NONE)
            found = jnp.maximum(found, jnp.max(part.reshape(STEP // 8, 8, STEP), axis=0))
        best[:, block] = found


def far_kernel(bounds, partials, unit, best, four, out):
    z, xl, core = lax.axis_index("z"), lax.axis_index("xl"), lax.axis_index("c")
    piece = normalizer(partials)(four[...])
    start = plane_start(z, xl, 4) + core * ROWS
    found = raise_best(best[...], bounds, unit, piece, start, z)
    found = jnp.max(found, axis=0, keepdims=True)
    for k in range(PLANE // 128):
        out[k // 2, pl.ds(k % 2, 1)] = found[:, k * 128 : (k + 1) * 128]


IN_VMEM = pl.BlockSpec(memory_space=pltpu.VMEM)
ANYWHERE = pl.BlockSpec(memory_space=pl.ANY)
PARAMS = pltpu.CompilerParams(vmem_limit_bytes=32 * 1024 * 1024)


def cost(flops):
    return pl.CostEstimate(flops=int(flops), bytes_accessed=4 * 2**20, transcendentals=0)


def near(bounds, partials, *blocks):
    return pl.pallas_call(
        near_kernel,
        out_shape=(
            jax.ShapeDtypeStruct((PLANE, D), jnp.bfloat16),
            jax.ShapeDtypeStruct((8, PLANE), jnp.float32),
        ),
        in_specs=[pl.BlockSpec(memory_space=pltpu.SMEM), IN_VMEM] + [ANYWHERE] * 6,
        out_specs=(IN_VMEM, IN_VMEM),
        scratch_shapes=[
            pltpu.VMEM((PLANE, D), jnp.bfloat16),
            pltpu.VMEM((ROWS + 3 * CHIP, D), jnp.bfloat16),
            pltpu.SemaphoreType.DMA((6,)),
        ],
        compiler_params=PARAMS,
        cost_estimate=cost(5e9),
        name="near",
    )(bounds, partials, *blocks)


def far(bounds, partials, unit, best, four):
    return pl.pallas_call(
        far_kernel,
        out_shape=jax.ShapeDtypeStruct((XL * C, ROWS // 128, 128), jnp.float32),
        in_specs=[pl.BlockSpec(memory_space=pltpu.SMEM)] + [IN_VMEM] * 4,
        out_specs=IN_VMEM,
        compiler_params=PARAMS,
        cost_estimate=cost(1e9),
        name="far",
    )(bounds, partials, unit, best, four)


def resend(received, count, flops):
    def kernel(received, out):
        total = jnp.sum(received[...], axis=0, keepdims=True)
        out[...] = jnp.broadcast_to(total, out.shape)

    return pl.pallas_call(
        kernel,
        out_shape=jax.ShapeDtypeStruct((count, 4, 128), jnp.float32),
        in_specs=[IN_VMEM],
        out_specs=IN_VMEM,
        compiler_params=pltpu.CompilerParams(vmem_limit_bytes=2 * 1024 * 1024),
        cost_estimate=cost(flops),
        name="resend",
    )(received)


def on_device(embeddings, cluster_rows):
    own = embeddings[0]
    chip = lax.all_gather(own, "c", axis=0, tiled=True)
    two = lax.ppermute(chip, ("z", "c"), shift((2, -2)))
    one = lax.ppermute(chip, ("z", "c"), shift((1, -1)))
    side = lax.ppermute(chip, "xl", [(0, 1), (1, 0)])
    column_sums = jnp.sum(chip, axis=0, dtype=jnp.float32).reshape(4, 128)
    sums = spread_sum(column_sums, ("xl", "y", "xh"), XL * Y * XH)
    three = lax.ppermute(two, ("z", "c"), shift((1, -1)))
    sums = resend(sums, Z, 8000000000)
    half = lax.dynamic_slice_in_dim(two, lax.axis_index("c") * ROWS, ROWS, 0)
    four = lax.ppermute(half, ("z", "c"), shift((2, -2)))
    partials = lax.all_to_all(sums, "z", 0, 0)
    unit, best = near(cluster_rows, partials, own, chip, side, two, one, three)
    best = far(cluster_rows, partials, unit, best, four)
    best = lax.all_to_all(best, ("xl", "c"), 0, 0)
    return jnp.max(best, axis=0).reshape(1, ROWS)


def solution(mesh):
    fine = Mesh(mesh.devices.reshape(Z, XL, C, Y, XH), (*GRP, *REP))
    inner = jax.shard_map(
        on_device,
        mesh=fine,
        in_specs=(P(REP, GRP, None), P(REP, None, None)),
        out_specs=P(REP, GRP),
        check_vma=False,
    )

    def run(embeddings, cluster_of, cluster_rows):
        del cluster_of
        return inner(embeddings, cluster_rows)

    return run
```

```python
import jax
import jax.numpy as jnp
from jax import lax
from jax.experimental import pallas as pl
from jax.experimental.pallas import tpu as pltpu
from jax.sharding import Mesh, PartitionSpec as P

Z, XL, C, Y, XH = 8, 2, 2, 8, 2
GRP = ("z", "xl", "c")
REP = ("y", "xh")
ROWS = 256
CHIP = C * ROWS
PLANE = XL * CHIP
D = 512
TOTAL = Z * PLANE * Y * XH
NONE = -2.0
STEP = 256


def shift(hops):
    return [(z * C + c, (z + hops[c]) % Z * C + c) for z in range(Z) for c in range(C)]


def spread_sum(partial, axes, count):
    return lax.all_to_all(jnp.broadcast_to(partial[None], (count, 4, 128)), axes, 0, 0)


def plane_start(z, xl, offset):
    return lax.rem(z + offset + Z, Z) * PLANE + xl * CHIP


def normalizer(partials):
    total = jnp.sum(partials[...], axis=0)
    centroid = jnp.concatenate([total[k : k + 1] for k in range(4)], axis=1) / TOTAL

    def normalized(block):
        centered = block.astype(jnp.float32) - centroid
        norm = jnp.sum(centered * centered, axis=1, keepdims=True)
        return (centered * lax.rsqrt(norm + 1e-06)).astype(jnp.bfloat16)

    return normalized


def cluster_by(bounds, position):
    member = jnp.zeros(position.shape, jnp.int32)
    for k in range(7):
        member += (position >= bounds[0, 1, k]).astype(jnp.int32)
    return member


def row_positions(z, xl):
    lane = lax.broadcasted_iota(jnp.int32, (1, PLANE), 1)
    return z * PLANE + jnp.where(lane < CHIP, xl * CHIP + lane, lane - xl * CHIP)


def near_kernel(bounds, partials, own, chip, side, two, one, three, unit, best, cols):
    z, xl, core = lax.axis_index("z"), lax.axis_index("xl"), lax.axis_index("c")
    sign = 2 * core - 1
    normalized = normalizer(partials)
    starts = [plane_start(z, xl, 0) + core * ROWS]
    cols[pl.ds(0, ROWS)] = normalized(own[...])
    for block, hops in ((two, 2), (one, 1), (three, 3)):
        for k in range(CHIP // STEP):
            cols[pl.ds(len(starts) * STEP, STEP)] = normalized(block[pl.ds(k * STEP, STEP)])
            starts.append(plane_start(z, xl, hops * sign) + k * STEP)
    offset = lax.broadcasted_iota(jnp.int32, (STEP, 1), 0)
    col_cluster = [cluster_by(bounds, start + offset) for start in starts]
    rows = row_positions(z, xl)
    row_cluster = cluster_by(bounds, rows)
    for k in range(PLANE // STEP):
        block = pl.ds(k * STEP, STEP)
        source = chip if k < CHIP // STEP else side
        slab = normalized(source[pl.ds(k * STEP % CHIP, STEP)])
        unit[block] = slab
        scores = lax.dot_general(
            cols[...], slab, (((1,), (1,)), ((), ())), preferred_element_type=jnp.float32
        )
        found = jnp.full((8, STEP), NONE, jnp.float32)
        for j, start in enumerate(starts):
            inside = col_cluster[j] == row_cluster[:, k * STEP : (k + 1) * STEP]
            if j == 0:
                inside &= start + offset != rows[:, k * STEP : (k + 1) * STEP]
            part = jnp.where(inside, scores[j * STEP : (j + 1) * STEP], NONE)
            found = jnp.maximum(found, jnp.max(part.reshape(STEP // 8, 8, STEP), axis=0))
        best[:, block] = found


def far_kernel(bounds, partials, unit, best, four, out):
    z, xl, core = lax.axis_index("z"), lax.axis_index("xl"), lax.axis_index("c")
    piece = normalizer(partials)(four[...])
    scores = lax.dot_general(
        piece, unit[...], (((1,), (1,)), ((), ())), preferred_element_type=jnp.float32
    )
    start = plane_start(z, xl, 4) + core * ROWS
    position = start + lax.broadcasted_iota(jnp.int32, (STEP, 1), 0)
    inside = cluster_by(bounds, position) == cluster_by(bounds, row_positions(z, xl))
    scores = jnp.where(inside, scores, NONE)
    found = jnp.maximum(best[...], jnp.max(scores.reshape(STEP // 8, 8, PLANE), axis=0))
    found = jnp.max(found, axis=0, keepdims=True)
    for k in range(PLANE // 128):
        device = lax.rem(2 * xl + k // 2, 4)
        out[device, pl.ds(k % 2, 1)] = found[:, k * 128 : (k + 1) * 128]


IN_VMEM = pl.BlockSpec(memory_space=pltpu.VMEM)
PARAMS = pltpu.CompilerParams(vmem_limit_bytes=32 * 1024 * 1024)


def cost(flops):
    return pl.CostEstimate(flops=int(flops), bytes_accessed=4 * 2**20, transcendentals=0)


def near(bounds, partials, *blocks):
    return pl.pallas_call(
        near_kernel,
        out_shape=(
            jax.ShapeDtypeStruct((PLANE, D), jnp.bfloat16),
            jax.ShapeDtypeStruct((8, PLANE), jnp.float32),
        ),
        in_specs=[pl.BlockSpec(memory_space=pltpu.SMEM)] + [IN_VMEM] * (1 + len(blocks)),
        out_specs=(IN_VMEM, IN_VMEM),
        scratch_shapes=[pltpu.VMEM((ROWS + 3 * CHIP, D), jnp.bfloat16)],
        compiler_params=PARAMS,
        cost_estimate=cost(5e9),
        name="near",
    )(bounds, partials, *blocks)


def far(bounds, partials, unit, best, four):
    return pl.pallas_call(
        far_kernel,
        out_shape=jax.ShapeDtypeStruct((XL * C, ROWS // 128, 128), jnp.float32),
        in_specs=[pl.BlockSpec(memory_space=pltpu.SMEM)] + [IN_VMEM] * 4,
        out_specs=IN_VMEM,
        compiler_params=PARAMS,
        cost_estimate=cost(1e9),
        name="far",
    )(bounds, partials, unit, best, four)


def resend(received, count, flops):
    def kernel(received, out):
        total = jnp.sum(received[...], axis=0, keepdims=True)
        out[...] = jnp.broadcast_to(total, out.shape)

    return pl.pallas_call(
        kernel,
        out_shape=jax.ShapeDtypeStruct((count, 4, 128), jnp.float32),
        in_specs=[IN_VMEM],
        out_specs=IN_VMEM,
        compiler_params=pltpu.CompilerParams(vmem_limit_bytes=2 * 1024 * 1024),
        cost_estimate=cost(flops),
        name="resend",
    )(received)


def on_device(embeddings, cluster_rows):
    own = embeddings[0]
    chip = lax.all_gather(own, "c", axis=0, tiled=True)
    two = lax.ppermute(chip, ("z", "c"), shift((2, -2)))
    one = lax.ppermute(chip, ("z", "c"), shift((1, -1)))
    side = lax.ppermute(chip, "xl", [(0, 1), (1, 0)])
    column_sums = jnp.sum(chip, axis=0, dtype=jnp.float32).reshape(4, 128)
    sums = spread_sum(column_sums, ("xl", "y", "xh"), XL * Y * XH)
    three = lax.ppermute(two, ("z", "c"), shift((1, -1)))
    sums = resend(sums, Z, 8000000000)
    half = lax.dynamic_slice_in_dim(two, lax.axis_index("c") * ROWS, ROWS, 0)
    four = lax.ppermute(half, ("z", "c"), shift((2, -2)))
    partials = lax.all_to_all(sums, "z", 0, 0)
    unit, best = near(cluster_rows, partials, own, chip, side, two, one, three)
    best = far(cluster_rows, partials, unit, best, four)
    best = lax.all_to_all(best, ("xl", "c"), 0, 0)
    return jnp.max(best, axis=0).reshape(1, ROWS)


def solution(mesh):
    fine = Mesh(mesh.devices.reshape(Z, XL, C, Y, XH), (*GRP, *REP))
    inner = jax.shard_map(
        on_device,
        mesh=fine,
        in_specs=(P(REP, GRP, None), P(REP, None, None)),
        out_specs=P(REP, GRP),
        check_vma=False,
    )

    def run(embeddings, cluster_of, cluster_rows):
        del cluster_of
        return inner(embeddings, cluster_rows)

    return run
```

```python
import jax
import jax.numpy as jnp
from jax import lax
from jax.experimental import pallas as pl
from jax.experimental.pallas import tpu as pltpu
from jax.sharding import Mesh, PartitionSpec as P

Z, XL, C, Y, XH = 8, 2, 2, 8, 2
GRP = ("z", "xl", "c")
REP = ("y", "xh")
ROWS = 256
CHIP = C * ROWS
PLANE = XL * CHIP
D = 512
TOTAL = Z * PLANE * Y * XH
NONE = -2.0
STEP = 256


def shift(hops):
    return [(z * C + c, (z + hops[c]) % Z * C + c) for z in range(Z) for c in range(C)]


def spread_sum(partial, axes, count):
    return lax.all_to_all(jnp.broadcast_to(partial[None], (count, 4, 128)), axes, 0, 0)


def plane_start(z, xl, offset):
    return lax.rem(z + offset + Z, Z) * PLANE + xl * CHIP


def normalizer(partials):
    total = jnp.sum(partials[...], axis=0)
    centroid = jnp.concatenate([total[k : k + 1] for k in range(4)], axis=1) / TOTAL

    def normalized(block):
        centered = block.astype(jnp.float32) - centroid
        norm = jnp.sum(centered * centered, axis=1, keepdims=True)
        return (centered * lax.rsqrt(norm + 1e-06)).astype(jnp.bfloat16)

    return normalized


def cluster_by(bounds, position):
    member = jnp.zeros(position.shape, jnp.int32)
    for k in range(7):
        member += (position >= bounds[0, 1, k]).astype(jnp.int32)
    return member


def row_positions(z, xl):
    lane = lax.broadcasted_iota(jnp.int32, (1, PLANE), 1)
    return z * PLANE + jnp.where(lane < CHIP, xl * CHIP + lane, lane - xl * CHIP)


def near_kernel(bounds, partials, own, chip, side, two, one, three, unit, best, cols):
    z, xl, core = lax.axis_index("z"), lax.axis_index("xl"), lax.axis_index("c")
    sign = 2 * core - 1
    normalized = normalizer(partials)
    starts = [plane_start(z, xl, 0) + core * ROWS]
    cols[pl.ds(0, ROWS)] = normalized(own[...])
    for block, hops in ((two, 2), (one, 1), (three, 3)):
        for k in range(CHIP // STEP):
            cols[pl.ds(len(starts) * STEP, STEP)] = normalized(block[pl.ds(k * STEP, STEP)])
            starts.append(plane_start(z, xl, hops * sign) + k * STEP)
    offset = lax.broadcasted_iota(jnp.int32, (STEP, 1), 0)
    col_cluster = [cluster_by(bounds, start + offset) for start in starts]
    rows = row_positions(z, xl)
    row_cluster = cluster_by(bounds, rows)
    for k in range(PLANE // STEP):
        block = pl.ds(k * STEP, STEP)
        source = chip if k < CHIP // STEP else side
        slab = normalized(source[pl.ds(k * STEP % CHIP, STEP)])
        unit[block] = slab
        scores = lax.dot_general(
            cols[...], slab, (((1,), (1,)), ((), ())), preferred_element_type=jnp.float32
        )
        found = jnp.full((8, STEP), NONE, jnp.float32)
        for j, start in enumerate(starts):
            inside = col_cluster[j] == row_cluster[:, k * STEP : (k + 1) * STEP]
            if j == 0:
                inside &= start + offset != rows[:, k * STEP : (k + 1) * STEP]
            part = jnp.where(inside, scores[j * STEP : (j + 1) * STEP], NONE)
            found = jnp.maximum(found, jnp.max(part.reshape(STEP // 8, 8, STEP), axis=0))
        best[:, block] = found


def far_kernel(bounds, partials, unit, best, four, out):
    z, xl, core = lax.axis_index("z"), lax.axis_index("xl"), lax.axis_index("c")
    piece = normalizer(partials)(four[...])
    scores = lax.dot_general(
        piece, unit[...], (((1,), (1,)), ((), ())), preferred_element_type=jnp.float32
    )
    start = plane_start(z, xl, 4) + core * ROWS
    position = start + lax.broadcasted_iota(jnp.int32, (STEP, 1), 0)
    inside = cluster_by(bounds, position) == cluster_by(bounds, row_positions(z, xl))
    scores = jnp.where(inside, scores, NONE)
    found = jnp.maximum(best[...], jnp.max(scores.reshape(STEP // 8, 8, PLANE), axis=0))
    found = jnp.max(found, axis=0, keepdims=True)
    for k in range(PLANE // 128):
        device = lax.rem(2 * xl + k // 2, 4)
        out[device, pl.ds(k % 2, 1)] = found[:, k * 128 : (k + 1) * 128]


IN_VMEM = pl.BlockSpec(memory_space=pltpu.VMEM)
PARAMS = pltpu.CompilerParams(vmem_limit_bytes=32 * 1024 * 1024)


def cost(flops):
    return pl.CostEstimate(flops=int(flops), bytes_accessed=4 * 2**20, transcendentals=0)


def near(bounds, partials, *blocks):
    return pl.pallas_call(
        near_kernel,
        out_shape=(
            jax.ShapeDtypeStruct((PLANE, D), jnp.bfloat16),
            jax.ShapeDtypeStruct((8, PLANE), jnp.float32),
        ),
        in_specs=[pl.BlockSpec(memory_space=pltpu.SMEM)] + [IN_VMEM] * (1 + len(blocks)),
        out_specs=(IN_VMEM, IN_VMEM),
        scratch_shapes=[pltpu.VMEM((ROWS + 3 * CHIP, D), jnp.bfloat16)],
        compiler_params=PARAMS,
        cost_estimate=cost(5e9),
        name="near",
    )(bounds, partials, *blocks)


def far(bounds, partials, unit, best, four):
    return pl.pallas_call(
        far_kernel,
        out_shape=jax.ShapeDtypeStruct((XL * C, ROWS // 128, 128), jnp.float32),
        in_specs=[pl.BlockSpec(memory_space=pltpu.SMEM)] + [IN_VMEM] * 4,
        out_specs=IN_VMEM,
        compiler_params=PARAMS,
        cost_estimate=cost(1e9),
        name="far",
    )(bounds, partials, unit, best, four)


def resend(received, count, flops):
    def kernel(received, out):
        total = jnp.sum(received[...], axis=0, keepdims=True)
        out[...] = jnp.broadcast_to(total, out.shape)

    return pl.pallas_call(
        kernel,
        out_shape=jax.ShapeDtypeStruct((count, 4, 128), jnp.float32),
        in_specs=[IN_VMEM],
        out_specs=IN_VMEM,
        compiler_params=pltpu.CompilerParams(vmem_limit_bytes=2 * 1024 * 1024),
        cost_estimate=cost(flops),
        name="resend",
    )(received)


def on_device(embeddings, cluster_rows):
    own = embeddings[0]
    chip = lax.all_gather(own, "c", axis=0, tiled=True)
    two = lax.ppermute(chip, ("z", "c"), shift((2, -2)))
    side = lax.ppermute(chip, "xl", [(0, 1), (1, 0)])
    column_sums = jnp.sum(chip, axis=0, dtype=jnp.float32).reshape(4, 128)
    sums = spread_sum(column_sums, ("xl", "y", "xh"), XL * Y * XH)
    later, two = lax.optimization_barrier((chip, two))
    one = lax.ppermute(later, ("z", "c"), shift((1, -1)))
    three = lax.ppermute(two, ("z", "c"), shift((1, -1)))
    sums = resend(sums, Z, 8000000000)
    half = lax.dynamic_slice_in_dim(three, lax.axis_index("c") * ROWS, ROWS, 0)
    four = lax.ppermute(half, ("z", "c"), shift((1, -1)))
    partials = lax.all_to_all(sums, "z", 0, 0)
    unit, best = near(cluster_rows, partials, own, chip, side, two, one, three)
    best = far(cluster_rows, partials, unit, best, four)
    best = lax.all_to_all(best, ("xl", "c"), 0, 0)
    return jnp.max(best, axis=0).reshape(1, ROWS)


def solution(mesh):
    fine = Mesh(mesh.devices.reshape(Z, XL, C, Y, XH), (*GRP, *REP))
    inner = jax.shard_map(
        on_device,
        mesh=fine,
        in_specs=(P(REP, GRP, None), P(REP, None, None)),
        out_specs=P(REP, GRP),
        check_vma=False,
    )

    def run(embeddings, cluster_of, cluster_rows):
        del cluster_of
        return inner(embeddings, cluster_rows)

    return run
```

```python
import jax
import jax.numpy as jnp
from jax import lax
from jax.experimental import pallas as pl
from jax.experimental.pallas import tpu as pltpu
from jax.sharding import Mesh, PartitionSpec as P

Z, XL, C, Y, XH = 8, 2, 2, 8, 2
GRP = ("z", "xl", "c")
REP = ("y", "xh")
ROWS = 256
CHIP = C * ROWS
PLANE = XL * CHIP
D = 512
TOTAL = Z * PLANE * Y * XH
NONE = -2.0
STEP = 256


def shift(hops):
    return [(z * C + c, (z + hops[c]) % Z * C + c) for z in range(Z) for c in range(C)]


def plane_start(z, xl, offset):
    return lax.rem(z + offset + Z, Z) * PLANE + xl * CHIP


def normalizer(partials):
    total = jnp.sum(partials[...], axis=0)
    centroid = jnp.concatenate([total[k : k + 1] for k in range(4)], axis=1) / TOTAL

    def normalized(block):
        centered = block.astype(jnp.float32) - centroid
        norm = jnp.sum(centered * centered, axis=1, keepdims=True)
        return (centered * lax.rsqrt(norm + 1e-06)).astype(jnp.bfloat16)

    return normalized


def cluster_by(bounds, position):
    member = jnp.zeros(position.shape, jnp.int32)
    for k in range(7):
        member += (position >= bounds[0, 1, k]).astype(jnp.int32)
    return member


def row_positions(z, xl):
    lane = lax.broadcasted_iota(jnp.int32, (1, PLANE), 1)
    return z * PLANE + jnp.where(lane < CHIP, xl * CHIP + lane, lane - xl * CHIP)


def near_kernel(bounds, partials, chip, side, two, one, three, unit, best, cols):
    z, xl, core = lax.axis_index("z"), lax.axis_index("xl"), lax.axis_index("c")
    sign = 2 * core - 1
    normalized = normalizer(partials)
    starts = [plane_start(z, xl, 0) + core * ROWS]
    cols[pl.ds(0, ROWS)] = normalized(chip[pl.ds(pl.multiple_of(core * ROWS, ROWS), ROWS)])
    for block, hops in ((two, 2), (one, 1), (three, 3)):
        for k in range(CHIP // STEP):
            cols[pl.ds(len(starts) * STEP, STEP)] = normalized(block[pl.ds(k * STEP, STEP)])
            starts.append(plane_start(z, xl, hops * sign) + k * STEP)
    offset = lax.broadcasted_iota(jnp.int32, (STEP, 1), 0)
    col_cluster = [cluster_by(bounds, start + offset) for start in starts]
    rows = row_positions(z, xl)
    row_cluster = cluster_by(bounds, rows)
    for k in range(PLANE // STEP):
        block = pl.ds(k * STEP, STEP)
        source = chip if k < CHIP // STEP else side
        slab = normalized(source[pl.ds(k * STEP % CHIP, STEP)])
        unit[block] = slab
        scores = lax.dot_general(
            cols[...], slab, (((1,), (1,)), ((), ())), preferred_element_type=jnp.float32
        )
        found = jnp.full((8, STEP), NONE, jnp.float32)
        for j, start in enumerate(starts):
            inside = col_cluster[j] == row_cluster[:, k * STEP : (k + 1) * STEP]
            if j == 0:
                inside &= start + offset != rows[:, k * STEP : (k + 1) * STEP]
            part = jnp.where(inside, scores[j * STEP : (j + 1) * STEP], NONE)
            found = jnp.maximum(found, jnp.max(part.reshape(STEP // 8, 8, STEP), axis=0))
        best[:, block] = found


def far_kernel(bounds, partials, unit, best, four, out):
    z, xl, core = lax.axis_index("z"), lax.axis_index("xl"), lax.axis_index("c")
    piece = normalizer(partials)(four[...])
    scores = lax.dot_general(
        piece, unit[...], (((1,), (1,)), ((), ())), preferred_element_type=jnp.float32
    )
    start = plane_start(z, xl, 4) + core * ROWS
    position = start + lax.broadcasted_iota(jnp.int32, (STEP, 1), 0)
    inside = cluster_by(bounds, position) == cluster_by(bounds, row_positions(z, xl))
    scores = jnp.where(inside, scores, NONE)
    found = jnp.maximum(best[...], jnp.max(scores.reshape(STEP // 8, 8, PLANE), axis=0))
    found = jnp.max(found, axis=0, keepdims=True)
    for k in range(PLANE // 128):
        device = lax.rem(2 * xl + k // 2, 4)
        out[device, pl.ds(k % 2, 1)] = found[:, k * 128 : (k + 1) * 128]


IN_VMEM = pl.BlockSpec(memory_space=pltpu.VMEM)
PARAMS = pltpu.CompilerParams(vmem_limit_bytes=32 * 1024 * 1024)


def cost(flops):
    return pl.CostEstimate(flops=int(flops), bytes_accessed=4 * 2**20, transcendentals=0)


def near(bounds, partials, *blocks):
    return pl.pallas_call(
        near_kernel,
        out_shape=(
            jax.ShapeDtypeStruct((PLANE, D), jnp.bfloat16),
            jax.ShapeDtypeStruct((8, PLANE), jnp.float32),
        ),
        in_specs=[pl.BlockSpec(memory_space=pltpu.SMEM)] + [IN_VMEM] * (1 + len(blocks)),
        out_specs=(IN_VMEM, IN_VMEM),
        scratch_shapes=[pltpu.VMEM((ROWS + 3 * CHIP, D), jnp.bfloat16)],
        compiler_params=PARAMS,
        cost_estimate=cost(5e9),
        name="near",
    )(bounds, partials, *blocks)


def far(bounds, partials, unit, best, four):
    return pl.pallas_call(
        far_kernel,
        out_shape=jax.ShapeDtypeStruct((XL * C, ROWS // 128, 128), jnp.float32),
        in_specs=[pl.BlockSpec(memory_space=pltpu.SMEM)] + [IN_VMEM] * 4,
        out_specs=IN_VMEM,
        compiler_params=PARAMS,
        cost_estimate=cost(1e9),
        name="far",
    )(bounds, partials, unit, best, four)


def resend(received, count, flops):
    def kernel(received, out):
        total = jnp.sum(received[...], axis=0, keepdims=True)
        out[...] = jnp.broadcast_to(total, out.shape)

    return pl.pallas_call(
        kernel,
        out_shape=jax.ShapeDtypeStruct((count, 4, 128), jnp.float32),
        in_specs=[IN_VMEM],
        out_specs=IN_VMEM,
        compiler_params=pltpu.CompilerParams(vmem_limit_bytes=2 * 1024 * 1024),
        cost_estimate=cost(flops),
        name="resend",
    )(received)


def first_sums(chip, count):
    def kernel(chip, out):
        total = jnp.sum(chip[...].astype(jnp.float32), axis=0, keepdims=True)
        parts = jnp.concatenate([total[:, k * 128 : (k + 1) * 128] for k in range(4)], axis=0)
        out[...] = jnp.broadcast_to(parts[None], out.shape)

    return pl.pallas_call(
        kernel,
        out_shape=jax.ShapeDtypeStruct((count, 4, 128), jnp.float32),
        in_specs=[IN_VMEM],
        out_specs=IN_VMEM,
        compiler_params=pltpu.CompilerParams(vmem_limit_bytes=4 * 1024 * 1024),
        cost_estimate=cost(1e8),
        name="first_sums",
    )(chip)


def on_device(embeddings, cluster_rows):
    chip = lax.all_gather(embeddings[0], "c", axis=0, tiled=True)
    two = lax.ppermute(chip, ("z", "c"), shift((2, -2)))
    side = lax.ppermute(chip, "xl", [(0, 1), (1, 0)])
    sums = lax.all_to_all(first_sums(chip, XL * Y * XH), ("xl", "y", "xh"), 0, 0)
    later, two = lax.optimization_barrier((chip, two))
    one = lax.ppermute(later, ("z", "c"), shift((1, -1)))
    three = lax.ppermute(two, ("z", "c"), shift((1, -1)))
    sums = resend(sums, Z, 8000000000)
    half = lax.dynamic_slice_in_dim(three, lax.axis_index("c") * ROWS, ROWS, 0)
    four = lax.ppermute(half, ("z", "c"), shift((1, -1)))
    partials = lax.all_to_all(sums, "z", 0, 0)
    unit, best = near(cluster_rows, partials, chip, side, two, one, three)
    best = far(cluster_rows, partials, unit, best, four)
    best = lax.all_to_all(best, ("xl", "c"), 0, 0)
    return jnp.max(best, axis=0).reshape(1, ROWS)


def solution(mesh):
    fine = Mesh(mesh.devices.reshape(Z, XL, C, Y, XH), (*GRP, *REP))
    inner = jax.shard_map(
        on_device,
        mesh=fine,
        in_specs=(P(REP, GRP, None), P(REP, None, None)),
        out_specs=P(REP, GRP),
        check_vma=False,
    )

    def run(embeddings, cluster_of, cluster_rows):
        del cluster_of
        return inner(embeddings, cluster_rows)

    return run
```
